32 devices in a mesh: groups: 2 (over y), aux: 4 (over x, core), pair: 4 (over z).
Axes of the slice: x: 2, y: 2, z: 4, core: 2. Of those that a mesh axis runs over, the one named last changes fastest.
Arguments:
- tile_values: bfloat16 [256, 64, 4096], P('pair', ('groups', 'aux')), parts along dimension 1, may hold values from -6 to 6
- tile_pairs: int32 [256, 2], P('pair'), may hold values from 0 to 319, as said below
- tile_counts: int32 [4], P('pair'), may hold values from 8 to 64, as said below
- coeffs: bfloat16 [20480, 32], P('pair', 'groups'), parts along dimension 1, may hold values from -0.25 to 0.25
- domains: int32 [32, 8], P('groups'), parts along dimension 0, may hold values from 0 to 319, as said below
- virtual: bfloat16 [32, 512, 256], P(('groups', 'pair', 'aux')), parts along dimension 0, may hold values from -0.25 to 0.25
Outputs:
- fitted: bfloat16 [16, 64, 256], P(('pair', 'aux'), 'groups'), parts along dimension 1
The draws below stay inside these ranges and needn't reach their ends.
There are 2 independent parts, one for each index of `groups`. The reference program is written for one: setup_inputs(seed, part) draws one part's arguments, and reference() takes and returns one part's arrays. A program takes and returns all parts, laid end to end along the dimension named above; an argument that names none is the same for every part. Nothing has to cross between parts.
Inputs may be any that keep to these rules, and one draw needn't show every extreme that they name: `tile_pairs`: the list of pair device p holds distinct pairs; every slot, live or not, has its mu block among that device's own blocks p * 80 to p * 80 + 79, and its nu block within 3 blocks of the mu block, cyclically modulo 320. Slots from the device's tile_counts entry on are padding. `tile_counts`: some device's list is full in every draw. `domains`: the domain of orbital i, listed in some order, is the cyclic run of 8 consecutive blocks modulo 320 that begins at a block from p * 80 to p * 80 + 79, where p = floor(i * 320 / 1280).
All inputs are finite; a program needn't handle non-finite values.
Results may differ from the reference program's by a relative error of at most 0.0051.
Values may be sent and summed in bfloat16 or wider, within the bound.
No kernel may reach another device: no remote copies, remote signals or barrier semaphores. Data moves between devices by JAX's collectives and lax.ppermute only.
A program may use at most 64 MiB of HBM per device.

```python
import jax
import jax.numpy as jnp
from jax import lax

NBLK = 320
DOM = 8
NVIRT = 256
TILES_DEV = 64
BLK_DEV = 80
NAO = 20480
NAUX = 32
ORBS = 16
TILES = 256
DOMW = 512
N_PAIR = 4


def screened_lists(key):
    devices = NBLK // BLK_DEV
    count_key, pick_key, spot_key = jax.random.split(key, 3)
    counts = jax.random.randint(count_key, (devices,), TILES_DEV // 8, TILES_DEV)
    spot = jax.random.randint(spot_key, (), 0, devices)
    counts = jnp.where(jnp.arange(devices) == spot, TILES_DEV, counts)
    candidates = BLK_DEV * 7
    list_keys = jax.random.split(pick_key, devices)
    orders = jax.vmap(lambda one_key: jax.random.permutation(one_key, candidates))(list_keys)
    first_row = orders[0]
    where_two = jnp.argmax(first_row == 2)
    first_row = first_row.at[where_two].set(first_row[0]).at[0].set(2)
    orders = orders.at[0].set(first_row)[:, :TILES_DEV]
    local_block = orders // 7
    offset = orders % 7 - 3
    mu_block = jnp.arange(devices)[:, None] * BLK_DEV + local_block
    nu_block = (mu_block + offset + NBLK) % NBLK
    pairs = jnp.stack([mu_block, nu_block], axis=-1).reshape(devices * TILES_DEV, 2)
    return (pairs.astype(jnp.int32), counts.astype(jnp.int32))


def draw_tile_pairs(key, part):
    pairs, counts = screened_lists(key)
    return pairs


def draw_tile_counts(key, part):
    pairs, counts = screened_lists(key)
    return counts


def draw_domains(key, part):
    key = jax.random.fold_in(key, 7)
    center_key, order_key = jax.random.split(key)
    devices = NBLK // BLK_DEV
    slab = ORBS // devices
    owner = jnp.arange(ORBS, dtype=jnp.int32)[:, None] // slab
    offsets = jax.random.randint(center_key, (ORBS, 1), 0, BLK_DEV)
    centers = owner * BLK_DEV + offsets
    centers = centers.at[ORBS - 1, 0].set(NBLK - 1)
    row_keys = jax.random.split(order_key, ORBS)
    orders = jax.vmap(lambda one_key: jax.random.permutation(one_key, DOM))(row_keys)
    return ((centers + orders) % NBLK).astype(jnp.int32)


def steps_of(key, extent, cuts, smallest, largest):
    def one(dim, blocks):
        heights = jax.random.uniform(jax.random.fold_in(jax.random.fold_in(key, 6), dim), (blocks,), jnp.float32, smallest / len(cuts), largest / len(cuts))
        return jnp.repeat(jnp.exp(heights), extent[dim] // blocks).reshape((-1,) + (1,) * (len(extent) - dim - 1))

    level = one(*cuts[0])
    for cut in cuts[1:]:
        level = level * one(*cut)
    return level


def bell_draw(rng, shape, spread, limit, cuts=(), kind=jnp.bfloat16):
    result = jax.random.normal(rng, shape, jnp.float32) * spread
    if len(cuts) > 0:
        result = steps_of(rng, shape, cuts, -0.22, 0.18) * result
    return jnp.clip(result, min=-limit, max=limit).astype(kind)


def setup_inputs(seed: int = 0, part: int = 0) -> dict:
    key_of = jax.random.split(jax.random.key(seed), 7)
    own_keys = jax.random.split(jax.random.fold_in(key_of[6], part), 7)
    tile_values = bell_draw(own_keys[0], (TILES, NAUX, 4096), 1.0, 6.0, ((0, 4), (1, 4)))
    tile_pairs = draw_tile_pairs(jax.random.fold_in(key_of[6], 71), part)
    tile_counts = draw_tile_counts(jax.random.fold_in(key_of[6], 71), part)
    coeffs = bell_draw(own_keys[3], (NAO, ORBS), (DOM * 64) ** -0.5, 0.25, ((0, 4),))
    domains = draw_domains(jax.random.fold_in(jax.random.fold_in(key_of[6], part), 71), part)
    virtual = bell_draw(own_keys[5], (ORBS, DOMW, NVIRT), (DOM * 64) ** -0.5, 0.25, ((0, 16),))
    return dict(tile_values=tile_values, tile_pairs=tile_pairs, tile_counts=tile_counts, coeffs=coeffs, domains=domains, virtual=virtual)


def reference(tile_values, tile_pairs, tile_counts, coeffs, domains, virtual):
    tiles_dev = tile_values.shape[0] // N_PAIR
    aux_count = tile_values.shape[1]
    orbitals = coeffs.shape[1]
    domain_len = domains.shape[1]
    block_count = coeffs.shape[0] // 64
    block_index = jnp.arange(block_count, dtype=jnp.int32)
    inside_mask = jnp.any(domains[None, :, :] == block_index[:, None, None], axis=2)
    masked = coeffs.reshape(block_count, 64, orbitals) * inside_mask[:, None, :].astype(jnp.bfloat16)
    all_values = tile_values.reshape(N_PAIR, tiles_dev, aux_count, 64, 64)
    all_pairs = tile_pairs.reshape(N_PAIR, tiles_dev, 2)
    slot_index = jnp.arange(tiles_dev, dtype=jnp.int32)
    domain_cols = domains.T

    def one_list(running, list_item):
        tile_block, pair_block, live_count = list_item
        live_mask = slot_index < live_count
        coef_rows = masked[pair_block[:, 0]].astype(jnp.float32)
        hit_mask = (domain_cols[None, :, :] == pair_block[:, 1][:, None, None]) & live_mask[:, None, None]
        weighted = coef_rows[:, :, None, :] * hit_mask[:, None, :, :].astype(jnp.float32)
        tile_term = jnp.einsum('tqmn,tmsi->iqsn', tile_block.astype(jnp.float32), weighted,
                               precision=lax.Precision.HIGHEST)
        return running + tile_term, None

    start_sum = jnp.zeros((orbitals, aux_count, domain_len, 64), jnp.float32)
    summed, unused = lax.scan(one_list, start_sum, (all_values, all_pairs, tile_counts))
    halfway = summed.reshape(orbitals, aux_count, domain_len * 64).astype(jnp.bfloat16)
    halfway = lax.optimization_barrier(halfway)
    fitted = jnp.einsum('iqk,ika->iqa', halfway.astype(jnp.float32), virtual.astype(jnp.float32),
                        precision=lax.Precision.HIGHEST)
    return fitted.astype(jnp.bfloat16)
```

```python
import functools

import jax
import jax.numpy as jnp
from jax import lax
from jax.experimental import pallas as pl
from jax.experimental.pallas import tpu as pltpu
from jax.sharding import PartitionSpec as P

BLOCK = 64
LANES = 128
MSG = jnp.float32


def half_kernel(sizes, count_s, pairs_hbm, dom_hbm, coef_hbm, tiles_hbm,
                own_keep, own_send, prior_keep, prior_send,
                pairs_v, dom_s, coef_v, coef_f, tiles_v, hits_v, hits_s,
                masks, picked, weights, sums, ctl_sems, tile_sems):
    slots, aux_dev, slab, domain_len, own_blocks, pair_size, chunks = sizes
    pair_id = lax.axis_index("pair")
    aux_id = lax.axis_index("aux")
    first_block = pair_id * own_blocks
    own_row = pair_id * slab
    prior_row = lax.rem(pair_id + pair_size - 1, pair_size) * slab
    half_rows = BLOCK // 2
    per_chunk = slots // chunks

    small = [
        pltpu.make_async_copy(dom_hbm, dom_s, ctl_sems.at[0]),
        pltpu.make_async_copy(pairs_hbm, pairs_v, ctl_sems.at[1]),
        pltpu.make_async_copy(coef_hbm, coef_v, ctl_sems.at[2]),
    ]
    for copy in small:
        copy.start()
    big = [
        pltpu.make_async_copy(
            tiles_hbm.at[pl.ds(k * per_chunk, per_chunk)],
            tiles_v.at[pl.ds(k * per_chunk, per_chunk)],
            tile_sems.at[k],
        )
        for k in range(chunks)
    ]
    for copy in big:
        copy.start()

    row_i = lax.broadcasted_iota(jnp.int32, (half_rows, LANES), 0)
    lane_i = lax.broadcasted_iota(jnp.int32, (half_rows, LANES), 1)
    for e in range(2):
        masks[e] = (lax.shift_right_arithmetic(lane_i - e * BLOCK, 1) == row_i).astype(jnp.float32)
    src = lax.broadcasted_iota(jnp.int32, (LANES, LANES), 0)
    dst = lax.broadcasted_iota(jnp.int32, (LANES, LANES), 1)
    spread = ((src & 1) == lax.shift_right_logical(dst, 6)).astype(jnp.bfloat16)
    sums[...] = jnp.zeros_like(sums)

    for copy in small[:2]:
        copy.wait()

    def orbital_row(i):
        return jnp.where(i < slab, own_row + i, prior_row + i - slab)

    slot_i = lax.broadcasted_iota(jnp.int32, (1, slots), 1)
    live = slot_i < count_s[0]
    mu = pairs_v[0:1, :]
    nu = pairs_v[1:2, :]
    any_hit = jnp.zeros((1, slots), jnp.int32)
    for i in range(2 * slab):
        row = orbital_row(i)
        at_mu = jnp.zeros((1, slots), jnp.int32)
        at_nu = jnp.zeros((1, slots), jnp.int32)
        for s in range(domain_len):
            block = dom_s[s, row]
            at_mu = jnp.where(mu == block, s + 1, at_mu)
            at_nu = jnp.where(nu == block, s + 1, at_nu)
        hit = live & (at_mu > 0) & (at_nu > 0)
        code = jnp.where(hit, at_mu * (domain_len + 1) + at_nu, 0)
        hits_v[i + 1:i + 2, 0:slots] = code
        any_hit = any_hit | code
    hits_v[0:1, 0:slots] = any_hit
    hits_copy = pltpu.make_async_copy(hits_v, hits_s, ctl_sems.at[0])
    hits_copy.start()

    small[2].wait()
    for e in range(own_blocks // 2):
        coef_f[e] = coef_v[:, e * LANES:(e + 1) * LANES].astype(jnp.float32)

    for i in range(2 * slab):
        row = orbital_row(i)
        for s in range(domain_len):
            local = jnp.clip(dom_s[s, row] - first_block, 0, own_blocks - 1)
            even = lax.shift_right_logical(local, 1)
            line = coef_f[even, pl.ds(row, 1), :]
            picked[pl.ds(s * half_rows, half_rows), :] = (masks[local & 1] * line).astype(jnp.bfloat16)
        weights[pl.ds(i * domain_len * half_rows, domain_len * half_rows), :] = jnp.dot(
            picked[...], spread, preferred_element_type=jnp.float32)

    hits_copy.wait()
    for copy in big:
        copy.wait()

    @pl.loop(0, slots)
    def _(t):
        @pl.when(hits_s[0, t] > 0)
        def _():
            @pl.loop(0, 2 * slab)
            def _(i):
                code = hits_s[i + 1, t]

                @pl.when(code > 0)
                def _():
                    at_mu = lax.div(code, domain_len + 1)
                    at_nu = code - at_mu * (domain_len + 1) - 1
                    base = (i * domain_len + at_mu - 1) * half_rows
                    total = jnp.zeros((aux_dev, LANES), jnp.float32)
                    for h in range(half_rows):
                        total += (tiles_v[t, :, h * LANES:(h + 1) * LANES].astype(jnp.float32)
                                  * weights[pl.ds(base + h, 1), :])
                    sums[i * domain_len + at_nu] += total

    low = lax.broadcasted_iota(jnp.int32, (aux_dev, LANES), 1) < BLOCK
    half = slab // 2

    def folded(i, u):
        left = sums[i * domain_len + 2 * u]
        right = sums[i * domain_len + 2 * u + 1]
        return jnp.where(low, left + pltpu.roll(left, BLOCK, 1), right + pltpu.roll(right, BLOCK, 1))

    for r in range(slab):
        target = lax.bitwise_xor(aux_id, r)
        for first, keep, send in ((0, own_keep, own_send), (slab, prior_keep, prior_send)):
            out = keep if r < half else send
            for u in range(domain_len // 2):
                out[r % half, :, u * LANES:(u + 1) * LANES] = folded(first + target, u).astype(out.dtype)


def half_blocks(tile_values, tile_pairs, tile_counts, coeffs, domains, slab, pair_size):
    slots, aux_dev, flat = tile_values.shape
    orbitals = coeffs.shape[1]
    domain_len = domains.shape[1]
    own_blocks = coeffs.shape[0] // BLOCK
    chunks = 8
    sizes = (slots, aux_dev, slab, domain_len, own_blocks, pair_size, chunks)
    out = jax.ShapeDtypeStruct((slab // 2, aux_dev, domain_len * BLOCK), MSG)
    any_spec = pl.BlockSpec(memory_space=pltpu.HBM)
    return pl.pallas_call(
        functools.partial(half_kernel, sizes),
        out_shape=[out] * 4,
        in_specs=[pl.BlockSpec(memory_space=pltpu.SMEM)] + [any_spec] * 4,
        out_specs=[pl.BlockSpec(memory_space=pltpu.VMEM)] * 4,
        scratch_shapes=[
            pltpu.VMEM((2, slots), jnp.int32),
            pltpu.SMEM((domain_len, orbitals), jnp.int32),
            pltpu.VMEM((orbitals, own_blocks * BLOCK), jnp.bfloat16),
            pltpu.VMEM((own_blocks * BLOCK // LANES, orbitals, LANES), jnp.float32),
            pltpu.VMEM((slots, aux_dev, flat), jnp.bfloat16),
            pltpu.VMEM(((2 * slab + 8) // 8 * 8, LANES), jnp.int32),
            pltpu.SMEM(((2 * slab + 8) // 8 * 8, LANES), jnp.int32),
            pltpu.VMEM((2, BLOCK // 2, LANES), jnp.float32),
            pltpu.VMEM((domain_len * BLOCK // 2, LANES), jnp.bfloat16),
            pltpu.VMEM((2 * slab * domain_len * BLOCK // 2, LANES), jnp.float32),
            pltpu.VMEM((2 * slab * domain_len, aux_dev, LANES), jnp.float32),
            pltpu.SemaphoreType.DMA((3,)),
            pltpu.SemaphoreType.DMA((chunks,)),
        ],
        compiler_params=pltpu.CompilerParams(vmem_limit_bytes=32 * 1024 * 1024),
    )(tile_counts, *[pltpu.with_memory_space_constraint(value, pltpu.HBM)
                     for value in (tile_pairs.T, domains.T, coeffs.T, tile_values)])


def moved(value, aux_mask, pair_step):
    aux_size, pair_size = lax.axis_size("aux"), lax.axis_size("pair")
    routes = [
        (a * pair_size + p, (a ^ aux_mask) * pair_size + (p + pair_step) % pair_size)
        for a in range(aux_size)
        for p in range(pair_size)
    ]
    return lax.ppermute(value, ("aux", "pair"), routes)


def fit_kernel(sources, *refs):
    count = 1 + max(max(ref for _, ref, _ in group) for group in sources)
    blocks = refs[:count]
    virtual, fitted, rows = refs[count:]
    aux_id = lax.axis_index("aux")
    height = blocks[0].shape[1]
    prior = {offset: (ref, place) for offset, ref, place in sources[1]}
    for offset, ref, place in sources[0]:
        ref_b, place_b = prior[offset]
        total = blocks[ref][place].astype(jnp.float32) + blocks[ref_b][place_b].astype(jnp.float32)
        start = pl.multiple_of(lax.bitwise_xor(aux_id, offset) * height, height)
        rows[pl.ds(start, height), :] = total
    fitted[0] = jnp.dot(rows[...].astype(jnp.bfloat16), virtual[0],
                        preferred_element_type=jnp.float32).astype(fitted.dtype)


def body(tile_values, tile_pairs, tile_counts, coeffs, domains, virtual):
    pair_size = lax.axis_size("pair")
    aux_size = lax.axis_size("aux")
    slab = coeffs.shape[1] // pair_size
    aux_dev = tile_values.shape[1]
    own_keep, own_send, prior_keep, prior_send = half_blocks(
        tile_values, tile_pairs, tile_counts, coeffs, domains, slab, pair_size)

    half = aux_size // 2
    mask = half | 1
    prior_here = moved(prior_keep, 1, -1)
    prior_there = moved(prior_send, mask, -1)
    own_there = moved(own_send, mask, 0)
    items = [(own_keep, 0, 0, 0), (own_there, 1, mask, 0), (prior_here, 1, 1, 1), (prior_there, 1, mask, 1)]
    while half > 2:
        part = half // 2
        mask = part | 1
        sent = moved(jnp.concatenate([item[0][part:] for item in items]), mask, 0)
        kept = [(value[:part], flip, source, kind) for value, flip, source, kind in items]
        got = [(sent[k * part:(k + 1) * part], flip ^ 1, source ^ mask, kind)
               for k, (_, flip, source, kind) in enumerate(items)]
        items = kept + got
        half = part
    last = moved(jnp.concatenate([value[1 - flip:2 - flip] for value, flip, _, _ in items]), 1, 0)
    sources = ([], [])
    for k, (_, flip, source, kind) in enumerate(items):
        sources[kind].append((source, k, flip))
        sources[kind].append((source ^ 1, len(items), k))
    arrays = [item[0] for item in items] + [last]
    return pl.pallas_call(
        functools.partial(fit_kernel, sources),
        out_shape=jax.ShapeDtypeStruct((1, aux_size * aux_dev, virtual.shape[2]), jnp.bfloat16),
        in_specs=[pl.BlockSpec(memory_space=pltpu.VMEM)] * (len(arrays) + 1),
        out_specs=pl.BlockSpec(memory_space=pltpu.VMEM),
        scratch_shapes=[pltpu.VMEM((aux_size * aux_dev, virtual.shape[1]), jnp.float32)],
        compiler_params=pltpu.CompilerParams(vmem_limit_bytes=16 * 1024 * 1024),
    )(*arrays, virtual)


def solution(mesh):
    placed = (
        P("pair", ("groups", "aux"), None),
        P("pair", None),
        P("pair"),
        P("pair", "groups"),
        P("groups", None),
        P(("groups", "pair", "aux"), None, None),
    )
    return jax.shard_map(
        body,
        mesh=mesh,
        in_specs=placed,
        out_specs=P(("pair", "aux"), "groups", None),
        check_vma=False,
    )
```

```python
import functools

import jax
import jax.numpy as jnp
from jax import lax
from jax.experimental import pallas as pl
from jax.experimental.pallas import tpu as pltpu
from jax.sharding import PartitionSpec as P

BLOCK = 64
LANES = 128
WORD = 32
UNROLL = 2
EARLY = 16


def half_kernel(sizes, count_s, pairs_hbm, dom_hbm, coef_hbm, tiles_hbm,
                own, prior,
                pairs_v, dom_s, coef_v, coef_f, tiles_v, hits_v, hits_s, found, todo,
                masks, picked, weights, sums, sems):
    slots, aux_dev, slab, domain_len, own_blocks, pair_size = sizes
    pair_id = lax.axis_index("pair")
    aux_id = lax.axis_index("aux")
    first_block = pair_id * own_blocks
    own_row = pair_id * slab
    prior_row = lax.rem(pair_id + pair_size - 1, pair_size) * slab
    half_rows = BLOCK // 2
    orbitals = 2 * slab

    small = [
        pltpu.make_async_copy(dom_hbm, dom_s, sems.at[0]),
        pltpu.make_async_copy(pairs_hbm, pairs_v, sems.at[1]),
        pltpu.make_async_copy(coef_hbm, coef_v, sems.at[2]),
    ]
    for copy in small:
        copy.start()
    early = pltpu.make_async_copy(
        tiles_hbm.at[pl.ds(0, EARLY)], tiles_v.at[pl.ds(0, EARLY)], sems.at[3])
    early.start()

    row_i = lax.broadcasted_iota(jnp.int32, (half_rows, LANES), 0)
    lane_i = lax.broadcasted_iota(jnp.int32, (half_rows, LANES), 1)
    for e in range(2):
        masks[e] = (lax.shift_right_arithmetic(lane_i - e * BLOCK, 1) == row_i).astype(jnp.float32)
    src = lax.broadcasted_iota(jnp.int32, (LANES, LANES), 0)
    dst = lax.broadcasted_iota(jnp.int32, (LANES, LANES), 1)
    spread = ((src & 1) == lax.shift_right_logical(dst, 6)).astype(jnp.bfloat16)
    sums[...] = jnp.zeros_like(sums)
    weights[pl.ds(orbitals * domain_len * half_rows, half_rows), :] = jnp.zeros((half_rows, LANES), jnp.float32)

    for copy in small[:2]:
        copy.wait()

    def orbital_row(i):
        return own_row + i if i < slab else prior_row + i - slab

    slot_i = lax.broadcasted_iota(jnp.int32, (1, slots), 1)
    live = slot_i < count_s[0]
    mu = pairs_v[0:1, :]
    nu = pairs_v[1:2, :]
    taken = jnp.zeros((1, slots), jnp.int32)
    coded = [jnp.zeros((1, slots), jnp.int32) for _ in range(orbitals)]
    for i in range(orbitals):
        row = orbital_row(i)
        at_mu = jnp.full((1, slots), -1, jnp.int32)
        at_nu = jnp.full((1, slots), -1, jnp.int32)
        for s in range(domain_len):
            block = dom_s[s, row]
            at_mu = jnp.where(mu == block, s, at_mu)
            at_nu = jnp.where(nu == block, s, at_nu)
        hit = live & (at_mu >= 0) & (at_nu >= 0)
        code = (i * domain_len + at_mu) * domain_len + at_nu
        for k in range(i + 1):
            coded[k] = jnp.where(hit & (taken == k), code, coded[k])
        taken = taken + hit.astype(jnp.int32)
    for k in range(orbitals):
        hits_v[k:k + 1, 0:slots] = coded[k]
    hits_v[orbitals:orbitals + 1, 0:slots] = taken
    hits_copy = pltpu.make_async_copy(hits_v, hits_s, sems.at[0])
    hits_copy.start()

    number = jnp.int32(0)
    early_number = number
    for first in range(0, slots, WORD):
        inside = (taken > 0) & (slot_i >= first) & (slot_i < first + WORD)
        word = jnp.sum(jnp.where(inside, lax.shift_left(1, slot_i & (WORD - 1)), 0))
        for t in range(WORD):
            if first + t == EARLY:
                early_number = number
            found[number] = first + t
            number = number + (lax.shift_right_logical(word, t) & 1)

    def tile_copy(t):
        return pltpu.make_async_copy(tiles_hbm.at[t], tiles_v.at[t], sems.at[4])

    @pl.loop(early_number, number)
    def _(j):
        tile_copy(found[j]).start()

    small[2].wait()
    for e in range(own_blocks // 2):
        coef_f[e] = coef_v[:, e * LANES:(e + 1) * LANES].astype(jnp.float32)

    for i in range(orbitals):
        row = orbital_row(i)
        for s in range(domain_len):
            local = jnp.clip(dom_s[s, row] - first_block, 0, own_blocks - 1)
            line = coef_f[lax.shift_right_logical(local, 1), pl.ds(row, 1), :]
            picked[pl.ds(s * half_rows, half_rows), :] = (masks[local & 1] * line).astype(jnp.bfloat16)
        weights[pl.ds(i * domain_len * half_rows, domain_len * half_rows), :] = jnp.dot(
            picked[...], spread, preferred_element_type=jnp.float32)

    hits_copy.wait()

    def listed(j, filled):
        t = found[j]

        def entry(k, at):
            todo[at] = hits_s[k, t] * slots + t
            return at + 1

        return lax.fori_loop(0, hits_s[orbitals, t], entry, filled)

    nothing = orbitals * domain_len * domain_len * slots
    early_hits = lax.fori_loop(0, early_number, listed, jnp.int32(0))
    for u in range(UNROLL - 1):
        todo[early_hits + u] = nothing
    early_steps = lax.div(early_hits + UNROLL - 1, UNROLL)
    hits = lax.fori_loop(early_number, number, listed, early_steps * UNROLL)
    for u in range(UNROLL - 1):
        todo[hits + u] = nothing
    steps = lax.div(hits + UNROLL - 1, UNROLL)

    def work(step):
        totals = []
        for u in range(UNROLL):
            word = todo[step * UNROLL + u]
            t = word & (slots - 1)
            code = lax.div(word, slots)
            at_nu = lax.rem(code, domain_len)
            source = lax.div(code, domain_len)
            base = source * half_rows
            target = lax.div(source, domain_len) * domain_len + at_nu
            parts = [None] * 4
            for h in range(half_rows):
                term = (tiles_v[t, :, h * LANES:(h + 1) * LANES].astype(jnp.float32)
                        * weights[pl.ds(base + h, 1), :])
                parts[h % 4] = term if parts[h % 4] is None else parts[h % 4] + term
            totals.append((target, (parts[0] + parts[1]) + (parts[2] + parts[3])))
        for target, total in totals:
            sums[target] += total

    early.wait()
    pl.loop(0, early_steps)(work)

    @pl.loop(early_number, number)
    def _(j):
        tile_copy(found[j]).wait()

    pl.loop(early_steps, steps)(work)

    low = lax.broadcasted_iota(jnp.int32, (aux_dev, LANES), 1) < BLOCK

    def folded(i, u):
        left = sums[i * domain_len + 2 * u]
        right = sums[i * domain_len + 2 * u + 1]
        return jnp.where(low, left + pltpu.roll(left, BLOCK, 1), right + pltpu.roll(right, BLOCK, 1))

    for r in range(slab):
        target = lax.bitwise_xor(aux_id, r)
        for first, out in ((0, own), (slab, prior)):
            for u in range(domain_len // 2):
                out[r, :, u * LANES:(u + 1) * LANES] = folded(first + target, u)


def half_blocks(tile_values, tile_pairs, tile_counts, coeffs, domains, slab, pair_size):
    slots, aux_dev, flat = tile_values.shape
    orbitals = coeffs.shape[1]
    domain_len = domains.shape[1]
    own_blocks = coeffs.shape[0] // BLOCK
    hits_rows = (2 * slab + 8) // 8 * 8
    sizes = (slots, aux_dev, slab, domain_len, own_blocks, pair_size)
    out = jax.ShapeDtypeStruct((slab, aux_dev, domain_len * BLOCK), jnp.float32)
    any_spec = pl.BlockSpec(memory_space=pltpu.HBM)
    return pl.pallas_call(
        functools.partial(half_kernel, sizes),
        out_shape=[out] * 2,
        in_specs=[pl.BlockSpec(memory_space=pltpu.SMEM)] + [any_spec] * 4,
        out_specs=[pl.BlockSpec(memory_space=pltpu.VMEM)] * 2,
        scratch_shapes=[
            pltpu.VMEM((2, slots), jnp.int32),
            pltpu.SMEM((domain_len, orbitals), jnp.int32),
            pltpu.VMEM((orbitals, own_blocks * BLOCK), jnp.bfloat16),
            pltpu.VMEM((own_blocks * BLOCK // LANES, orbitals, LANES), jnp.float32),
            pltpu.VMEM((slots, aux_dev, flat), jnp.bfloat16),
            pltpu.VMEM((hits_rows, LANES), jnp.int32),
            pltpu.SMEM((hits_rows, LANES), jnp.int32),
            pltpu.SMEM((slots + 1,), jnp.int32),
            pltpu.SMEM((2 * slab * slots + 2 * UNROLL,), jnp.int32),
            pltpu.VMEM((2, BLOCK // 2, LANES), jnp.float32),
            pltpu.VMEM((domain_len * BLOCK // 2, LANES), jnp.bfloat16),
            pltpu.VMEM(((2 * slab * domain_len + 1) * BLOCK // 2, LANES), jnp.float32),
            pltpu.VMEM((2 * slab * domain_len + 1, aux_dev, LANES), jnp.float32),
            pltpu.SemaphoreType.DMA((5,)),
        ],
        compiler_params=pltpu.CompilerParams(vmem_limit_bytes=32 * 1024 * 1024),
    )(tile_counts, *[pltpu.with_memory_space_constraint(value, pltpu.HBM)
                     for value in (tile_pairs.T, domains.T, coeffs.T, tile_values)])


def moved(value, aux_mask, pair_step):
    aux_size, pair_size = lax.axis_size("aux"), lax.axis_size("pair")
    routes = [
        (a * pair_size + p, (a ^ aux_mask) * pair_size + (p + pair_step) % pair_size)
        for a in range(aux_size)
        for p in range(pair_size)
    ]
    return lax.ppermute(value, ("aux", "pair"), routes)


def fit_kernel(sources, *refs):
    count = len(refs) - 3
    virtual, fitted, rows = refs[count:]
    aux_id = lax.axis_index("aux")
    height = refs[0].shape[1]
    for offset, ref, place in sources:
        start = pl.multiple_of(lax.bitwise_xor(aux_id, offset) * height, height)
        rows[pl.ds(start, height), :] = refs[ref][place].astype(jnp.float32)
    fitted[0] = jnp.dot(rows[...].astype(jnp.bfloat16), virtual[0],
                        preferred_element_type=jnp.float32).astype(fitted.dtype)


def body(tile_values, tile_pairs, tile_counts, coeffs, domains, virtual):
    pair_size = lax.axis_size("pair")
    aux_size = lax.axis_size("aux")
    slab = coeffs.shape[1] // pair_size
    aux_dev = tile_values.shape[1]
    own, prior = half_blocks(tile_values, tile_pairs, tile_counts, coeffs, domains, slab, pair_size)
    blocks = (own + moved(prior, 0, -1)).astype(jnp.bfloat16)

    items = [(blocks, 0, 0)]
    half = aux_size
    while half > 2:
        half //= 2
        mask = half | 1
        sent = moved(jnp.concatenate([value[half:] for value, _, _ in items]), mask, 0)
        kept = [(value[:half], flip, source) for value, flip, source in items]
        got = [(sent[k * half:(k + 1) * half], flip ^ 1, source ^ mask) for k, (_, flip, source) in enumerate(items)]
        items = kept + got
    last = moved(jnp.concatenate([value[1 - flip:2 - flip] for value, flip, _ in items]), 1, 0)
    sources = []
    for k, (_, flip, source) in enumerate(items):
        sources.append((source, k, flip))
        sources.append((source ^ 1, len(items), k))
    arrays = [item[0] for item in items] + [last]
    return pl.pallas_call(
        functools.partial(fit_kernel, sources),
        out_shape=jax.ShapeDtypeStruct((1, aux_size * aux_dev, virtual.shape[2]), jnp.bfloat16),
        in_specs=[pl.BlockSpec(memory_space=pltpu.VMEM)] * (len(arrays) + 1),
        out_specs=pl.BlockSpec(memory_space=pltpu.VMEM),
        scratch_shapes=[pltpu.VMEM((aux_size * aux_dev, virtual.shape[1]), jnp.float32)],
        compiler_params=pltpu.CompilerParams(vmem_limit_bytes=16 * 1024 * 1024),
    )(*arrays, virtual)


def solution(mesh):
    placed = (
        P("pair", ("groups", "aux"), None),
        P("pair", None),
        P("pair"),
        P("pair", "groups"),
        P("groups", None),
        P(("groups", "pair", "aux"), None, None),
    )
    return jax.shard_map(
        body,
        mesh=mesh,
        in_specs=placed,
        out_specs=P(("pair", "aux"), "groups", None),
        check_vma=False,
    )
```

```python
import functools

import jax
import jax.numpy as jnp
from jax import lax
from jax.experimental import pallas as pl
from jax.experimental.pallas import tpu as pltpu
from jax.sharding import PartitionSpec as P

BLOCK = 64
LANES = 128
WORD = 32
UNROLL = 2
EARLY = 32
CHUNK = 4


def half_kernel(sizes, count_s, pairs_hbm, dom_hbm, coef_hbm, tiles_hbm,
                own_keep, own_send, prior_keep, prior_send,
                pairs_v, dom_s, coef_v, coef_f, tiles_v, hits_v, hits_s, found, todo,
                masks, picked, weights, sums, sems):
    slots, aux_dev, slab, domain_len, own_blocks, pair_size = sizes
    pair_id = lax.axis_index("pair")
    aux_id = lax.axis_index("aux")
    first_block = pair_id * own_blocks
    own_row = pair_id * slab
    prior_row = lax.rem(pair_id + pair_size - 1, pair_size) * slab
    half_rows = BLOCK // 2
    orbitals = 2 * slab

    small = [
        pltpu.make_async_copy(dom_hbm, dom_s, sems.at[0]),
        pltpu.make_async_copy(pairs_hbm, pairs_v, sems.at[1]),
        pltpu.make_async_copy(coef_hbm, coef_v, sems.at[2]),
    ]
    for copy in small:
        copy.start()
    for first in range(0, EARLY, CHUNK):
        pltpu.make_async_copy(
            tiles_hbm.at[pl.ds(first, CHUNK)], tiles_v.at[pl.ds(first, CHUNK)], sems.at[3]).start()

    row_i = lax.broadcasted_iota(jnp.int32, (half_rows, LANES), 0)
    lane_i = lax.broadcasted_iota(jnp.int32, (half_rows, LANES), 1)
    for e in range(2):
        masks[e] = (lax.shift_right_arithmetic(lane_i - e * BLOCK, 1) == row_i).astype(jnp.float32)
    src = lax.broadcasted_iota(jnp.int32, (LANES, LANES), 0)
    dst = lax.broadcasted_iota(jnp.int32, (LANES, LANES), 1)
    spread = ((src & 1) == lax.shift_right_logical(dst, 6)).astype(jnp.bfloat16)
    sums[...] = jnp.zeros_like(sums)
    weights[pl.ds(orbitals * domain_len * half_rows, half_rows), :] = jnp.zeros((half_rows, LANES), jnp.float32)

    for copy in small[:2]:
        copy.wait()

    def orbital_row(i):
        return own_row + i if i < slab else prior_row + i - slab

    slot_i = lax.broadcasted_iota(jnp.int32, (1, slots), 1)
    live = slot_i < count_s[0]
    mu = pairs_v[0:1, :]
    nu = pairs_v[1:2, :]
    taken = jnp.zeros((1, slots), jnp.int32)
    coded = [jnp.zeros((1, slots), jnp.int32) for _ in range(orbitals)]
    for i in range(orbitals):
        row = orbital_row(i)
        at_mu = jnp.full((1, slots), -1, jnp.int32)
        at_nu = jnp.full((1, slots), -1, jnp.int32)
        for s in range(domain_len):
            block = dom_s[s, row]
            at_mu = jnp.where(mu == block, s, at_mu)
            at_nu = jnp.where(nu == block, s, at_nu)
        hit = live & (at_mu >= 0) & (at_nu >= 0)
        code = (i * domain_len + at_mu) * domain_len + at_nu
        for k in range(i + 1):
            coded[k] = jnp.where(hit & (taken == k), code, coded[k])
        taken = taken + hit.astype(jnp.int32)
    for k in range(orbitals):
        hits_v[k:k + 1, 0:slots] = coded[k]
    hits_v[orbitals:orbitals + 1, 0:slots] = taken
    hits_copy = pltpu.make_async_copy(hits_v, hits_s, sems.at[0])
    hits_copy.start()

    number = jnp.int32(0)
    early_number = number
    for first in range(0, slots, WORD):
        inside = (taken > 0) & (slot_i >= first) & (slot_i < first + WORD)
        word = jnp.sum(jnp.where(inside, lax.shift_left(1, slot_i & (WORD - 1)), 0))
        for t in range(WORD):
            if first + t == EARLY:
                early_number = number
            found[number] = first + t
            number = number + (lax.shift_right_logical(word, t) & 1)

    def tile_copy(t):
        return pltpu.make_async_copy(tiles_hbm.at[t], tiles_v.at[t], sems.at[4])

    @pl.loop(early_number, number)
    def _(j):
        tile_copy(found[j]).start()

    small[2].wait()
    for e in range(own_blocks // 2):
        coef_f[e] = coef_v[:, e * LANES:(e + 1) * LANES].astype(jnp.float32)

    for i in range(orbitals):
        row = orbital_row(i)
        for s in range(domain_len):
            local = jnp.clip(dom_s[s, row] - first_block, 0, own_blocks - 1)
            line = coef_f[lax.shift_right_logical(local, 1), pl.ds(row, 1), :]
            picked[pl.ds(s * half_rows, half_rows), :] = (masks[local & 1] * line).astype(jnp.bfloat16)
        weights[pl.ds(i * domain_len * half_rows, domain_len * half_rows), :] = jnp.dot(
            picked[...], spread, preferred_element_type=jnp.float32)

    hits_copy.wait()

    def listed(j, filled):
        t = found[j]

        def entry(k, at):
            todo[at] = hits_s[k, t] * slots + t
            return at + 1

        return lax.fori_loop(0, hits_s[orbitals, t], entry, filled)

    nothing = orbitals * domain_len * domain_len * slots
    early_hits = lax.fori_loop(0, early_number, listed, jnp.int32(0))
    for u in range(UNROLL - 1):
        todo[early_hits + u] = nothing
    early_steps = lax.div(early_hits + UNROLL - 1, UNROLL)
    hits = lax.fori_loop(early_number, number, listed, early_steps * UNROLL)
    for u in range(UNROLL - 1):
        todo[hits + u] = nothing
    steps = lax.div(hits + UNROLL - 1, UNROLL)

    def work(step):
        totals = []
        for u in range(UNROLL):
            word = todo[step * UNROLL + u]
            t = word & (slots - 1)
            code = lax.div(word, slots)
            at_nu = lax.rem(code, domain_len)
            source = lax.div(code, domain_len)
            base = source * half_rows
            target = lax.div(source, domain_len) * domain_len + at_nu
            parts = [None] * 4
            for h in range(half_rows):
                term = (tiles_v[t, :, h * LANES:(h + 1) * LANES].astype(jnp.float32)
                        * weights[pl.ds(base + h, 1), :])
                parts[h % 4] = term if parts[h % 4] is None else parts[h % 4] + term
            totals.append((target, (parts[0] + parts[1]) + (parts[2] + parts[3])))
        for target, total in totals:
            sums[target] += total

    pltpu.make_async_copy(tiles_hbm.at[pl.ds(0, EARLY)], tiles_v.at[pl.ds(0, EARLY)], sems.at[3]).wait()
    pl.loop(0, early_steps)(work)

    @pl.loop(early_number, number)
    def _(j):
        tile_copy(found[j]).wait()

    pl.loop(early_steps, steps)(work)

    fold(slab, domain_len, aux_id, lambda k: sums[slab * domain_len + k], prior_keep, prior_send)
    fold(slab, domain_len, aux_id, lambda k: sums[k], own_keep, own_send)


def fold(slab, domain_len, aux_id, read, keep, send):
    half = slab // 2
    for r in range(slab):
        first = lax.bitwise_xor(aux_id, r) * domain_len
        out = keep if r < half else send
        for u in range(domain_len // 2):
            left, right = read(first + 2 * u), read(first + 2 * u + 1)
            low = lax.broadcasted_iota(jnp.int32, left.shape, 1) < BLOCK
            out[r % half, :, u * LANES:(u + 1) * LANES] = (
                jnp.where(low, left, right) + pltpu.roll(jnp.where(low, right, left), BLOCK, 1)).astype(out.dtype)


def half_blocks(tile_values, tile_pairs, tile_counts, coeffs, domains, slab, pair_size):
    slots, aux_dev, flat = tile_values.shape
    orbitals = coeffs.shape[1]
    domain_len = domains.shape[1]
    own_blocks = coeffs.shape[0] // BLOCK
    hits_rows = (2 * slab + 8) // 8 * 8
    sizes = (slots, aux_dev, slab, domain_len, own_blocks, pair_size)
    out = jax.ShapeDtypeStruct((slab // 2, aux_dev, domain_len * BLOCK), jnp.float32)
    thin = jax.ShapeDtypeStruct(out.shape, jnp.bfloat16)
    vmem_spec = pl.BlockSpec(memory_space=pltpu.VMEM)
    any_spec = pl.BlockSpec(memory_space=pltpu.HBM)
    return pl.pallas_call(
        functools.partial(half_kernel, sizes),
        out_shape=[out, thin, thin, thin],
        in_specs=[pl.BlockSpec(memory_space=pltpu.SMEM)] + [any_spec] * 4,
        out_specs=[vmem_spec] * 4,
        scratch_shapes=[
            pltpu.VMEM((2, slots), jnp.int32),
            pltpu.SMEM((domain_len, orbitals), jnp.int32),
            pltpu.VMEM((orbitals, own_blocks * BLOCK), jnp.bfloat16),
            pltpu.VMEM((own_blocks * BLOCK // LANES, orbitals, LANES), jnp.float32),
            pltpu.VMEM((slots, aux_dev, flat), jnp.bfloat16),
            pltpu.VMEM((hits_rows, LANES), jnp.int32),
            pltpu.SMEM((hits_rows, LANES), jnp.int32),
            pltpu.SMEM((slots + 1,), jnp.int32),
            pltpu.SMEM((2 * slab * slots + 2 * UNROLL,), jnp.int32),
            pltpu.VMEM((2, BLOCK // 2, LANES), jnp.float32),
            pltpu.VMEM((domain_len * BLOCK // 2, LANES), jnp.bfloat16),
            pltpu.VMEM(((2 * slab * domain_len + 1) * BLOCK // 2, LANES), jnp.float32),
            pltpu.VMEM((2 * slab * domain_len + 1, aux_dev, LANES), jnp.float32),
            pltpu.SemaphoreType.DMA((5,)),
        ],
        compiler_params=pltpu.CompilerParams(vmem_limit_bytes=16 * 1024 * 1024),
    )(tile_counts, *[pltpu.with_memory_space_constraint(value, pltpu.HBM)
                     for value in (tile_pairs.T, domains.T, coeffs.T, tile_values)])


def moved(value, aux_mask, pair_step):
    aux_size, pair_size = lax.axis_size("aux"), lax.axis_size("pair")
    routes = [
        (a * pair_size + p, (a ^ aux_mask) * pair_size + (p + pair_step) % pair_size)
        for a in range(aux_size)
        for p in range(pair_size)
    ]
    return lax.ppermute(value, ("aux", "pair"), routes)


def fit_kernel(sources, *refs):
    count = len(refs) - 3
    virtual, fitted, rows = refs[count:]
    aux_id = lax.axis_index("aux")
    height = refs[0].shape[1]
    for offset, ref, place in sources:
        start = pl.multiple_of(lax.bitwise_xor(aux_id, offset) * height, height)
        rows[pl.ds(start, height), :] = refs[ref][place].astype(jnp.float32)
    fitted[0] = jnp.dot(rows[...].astype(jnp.bfloat16), virtual[0],
                        preferred_element_type=jnp.float32).astype(fitted.dtype)


def body(tile_values, tile_pairs, tile_counts, coeffs, domains, virtual):
    pair_size = lax.axis_size("pair")
    aux_size = lax.axis_size("aux")
    slab = coeffs.shape[1] // pair_size
    aux_dev = tile_values.shape[1]
    own_keep, own_send, prior_keep, prior_send = half_blocks(tile_values, tile_pairs, tile_counts, coeffs, domains, slab, pair_size)

    half = aux_size // 2
    mask = half | 1
    prior_here = moved(prior_keep, 0, -1)
    prior_there = moved(prior_send, mask, -1)
    own_there = moved(own_send, mask, 0)
    prior_there, prior_here = lax.optimization_barrier((prior_there, prior_here))
    items = [((prior_here.astype(jnp.float32) + own_keep).astype(jnp.bfloat16), 0, 0),
             ((prior_there.astype(jnp.float32) + own_there.astype(jnp.float32)).astype(jnp.bfloat16), 1, mask)]
    while half > 2:
        half //= 2
        mask = half | 1
        sent = moved(jnp.concatenate([value[half:] for value, _, _ in items]), mask, 0)
        kept = [(value[:half], flip, source) for value, flip, source in items]
        got = [(sent[k * half:(k + 1) * half], flip ^ 1, source ^ mask) for k, (_, flip, source) in enumerate(items)]
        items = kept + got
    last = moved(jnp.concatenate([value[1 - flip:2 - flip] for value, flip, _ in items]), 1, 0)
    sources = []
    for k, (_, flip, source) in enumerate(items):
        sources.append((source, k, flip))
        sources.append((source ^ 1, len(items), k))
    arrays = [item[0] for item in items] + [last]
    return pl.pallas_call(
        functools.partial(fit_kernel, sources),
        out_shape=jax.ShapeDtypeStruct((1, aux_size * aux_dev, virtual.shape[2]), jnp.bfloat16),
        in_specs=[pl.BlockSpec(memory_space=pltpu.VMEM)] * (len(arrays) + 1),
        out_specs=pl.BlockSpec(memory_space=pltpu.VMEM),
        scratch_shapes=[pltpu.VMEM((aux_size * aux_dev, virtual.shape[1]), jnp.float32)],
        compiler_params=pltpu.CompilerParams(vmem_limit_bytes=4 * 1024 * 1024),
    )(*arrays, virtual)


def solution(mesh):
    placed = (
        P("pair", ("groups", "aux"), None),
        P("pair", None),
        P("pair"),
        P("pair", "groups"),
        P("groups", None),
        P(("groups", "pair", "aux"), None, None),
    )
    return jax.shard_map(
        body,
        mesh=mesh,
        in_specs=placed,
        out_specs=P(("pair", "aux"), "groups", None),
        check_vma=False,
    )
```

```python
import functools

import jax
import jax.numpy as jnp
from jax import lax
from jax.experimental import pallas as pl
from jax.experimental.pallas import tpu as pltpu
from jax.sharding import PartitionSpec as P

BLOCK = 64
LANES = 128
WORD = 32
UNROLL = 2
EARLY = 32
CHUNK = 4


def half_terms(sizes, orbitals, with_own, count_s, pairs_hbm, dom_hbm, coef_hbm, tiles_hbm,
               pairs_v, dom_s, coef_v, coef_f, tiles_v, hits_v, hits_s, found, todo,
               masks, picked, weights, sums, sems):
    slots, aux_dev, slab, domain_len, own_blocks, pair_size = sizes
    pair_id = lax.axis_index("pair")
    first_block = pair_id * own_blocks
    own_row = pair_id * slab
    prior_row = lax.rem(pair_id + pair_size - 1, pair_size) * slab
    half_rows = BLOCK // 2

    small = [
        pltpu.make_async_copy(dom_hbm, dom_s, sems.at[0]),
        pltpu.make_async_copy(pairs_hbm, pairs_v, sems.at[1]),
        pltpu.make_async_copy(coef_hbm, coef_v, sems.at[2]),
    ]
    for copy in small:
        copy.start()
    @pl.when(with_own)
    def _():
        for first in range(0, EARLY, CHUNK):
            pltpu.make_async_copy(
                tiles_hbm.at[pl.ds(first, CHUNK)], tiles_v.at[pl.ds(first, CHUNK)], sems.at[3]).start()


    row_i = lax.broadcasted_iota(jnp.int32, (half_rows, LANES), 0)
    lane_i = lax.broadcasted_iota(jnp.int32, (half_rows, LANES), 1)
    for e in range(2):
        masks[e] = (lax.shift_right_arithmetic(lane_i - e * BLOCK, 1) == row_i).astype(jnp.float32)
    src = lax.broadcasted_iota(jnp.int32, (LANES, LANES), 0)
    dst = lax.broadcasted_iota(jnp.int32, (LANES, LANES), 1)
    spread = ((src & 1) == lax.shift_right_logical(dst, 6)).astype(jnp.bfloat16)
    sums[...] = jnp.zeros_like(sums)
    weights[pl.ds(orbitals * domain_len * half_rows, half_rows), :] = jnp.zeros((half_rows, LANES), jnp.float32)

    for copy in small[:2]:
        copy.wait()

    def orbital_row(i):
        return own_row + i if i < slab else prior_row + i - slab

    slot_i = lax.broadcasted_iota(jnp.int32, (1, slots), 1)
    live = slot_i < count_s[0]
    mu = pairs_v[0:1, :]
    nu = pairs_v[1:2, :]
    taken = jnp.zeros((1, slots), jnp.int32)
    coded = [jnp.zeros((1, slots), jnp.int32) for _ in range(orbitals)]
    for i in range(orbitals):
        row = orbital_row(i)
        at_mu = jnp.full((1, slots), -1, jnp.int32)
        at_nu = jnp.full((1, slots), -1, jnp.int32)
        for s in range(domain_len):
            block = dom_s[s, row]
            at_mu = jnp.where(mu == block, s, at_mu)
            at_nu = jnp.where(nu == block, s, at_nu)
        hit = (live & with_own if i < slab else live) & (at_mu >= 0) & (at_nu >= 0)
        code = (i * domain_len + at_mu) * domain_len + at_nu
        for k in range(i + 1):
            coded[k] = jnp.where(hit & (taken == k), code, coded[k])
        taken = taken + hit.astype(jnp.int32)
    for k in range(orbitals):
        hits_v[k:k + 1, 0:slots] = coded[k]
    hits_v[orbitals:orbitals + 1, 0:slots] = taken
    hits_copy = pltpu.make_async_copy(hits_v, hits_s, sems.at[0])
    hits_copy.start()

    number = jnp.int32(0)
    early_number = number
    for first in range(0, slots, WORD):
        inside = (taken > 0) & (slot_i >= first) & (slot_i < first + WORD)
        word = jnp.sum(jnp.where(inside, lax.shift_left(1, slot_i & (WORD - 1)), 0))
        for t in range(WORD):
            if first + t == EARLY:
                early_number = number
            found[number] = first + t
            number = number + (lax.shift_right_logical(word, t) & 1)

    early_number = jnp.where(with_own, early_number, 0)

    def tile_copy(t):
        return pltpu.make_async_copy(tiles_hbm.at[t], tiles_v.at[t], sems.at[4])

    @pl.loop(early_number, number)
    def _(j):
        tile_copy(found[j]).start()

    small[2].wait()
    for e in range(own_blocks // 2):
        coef_f[e] = coef_v[:, e * LANES:(e + 1) * LANES].astype(jnp.float32)

    for i in range(orbitals):
        row = orbital_row(i)
        for s in range(domain_len):
            local = jnp.clip(dom_s[s, row] - first_block, 0, own_blocks - 1)
            line = coef_f[lax.shift_right_logical(local, 1), pl.ds(row, 1), :]
            picked[pl.ds(s * half_rows, half_rows), :] = (masks[local & 1] * line).astype(jnp.bfloat16)
        weights[pl.ds(i * domain_len * half_rows, domain_len * half_rows), :] = jnp.dot(
            picked[...], spread, preferred_element_type=jnp.float32)

    hits_copy.wait()

    def listed(j, filled):
        t = found[j]

        def entry(k, at):
            todo[at] = hits_s[k, t] * slots + t
            return at + 1

        return lax.fori_loop(0, hits_s[orbitals, t], entry, filled)

    nothing = orbitals * domain_len * domain_len * slots
    early_hits = lax.fori_loop(0, early_number, listed, jnp.int32(0))
    for u in range(UNROLL - 1):
        todo[early_hits + u] = nothing
    early_steps = lax.div(early_hits + UNROLL - 1, UNROLL)
    hits = lax.fori_loop(early_number, number, listed, early_steps * UNROLL)
    for u in range(UNROLL - 1):
        todo[hits + u] = nothing
    steps = lax.div(hits + UNROLL - 1, UNROLL)

    def work(step):
        totals = []
        for u in range(UNROLL):
            word = todo[step * UNROLL + u]
            t = word & (slots - 1)
            code = lax.div(word, slots)
            at_nu = lax.rem(code, domain_len)
            source = lax.div(code, domain_len)
            base = source * half_rows
            target = lax.div(source, domain_len) * domain_len + at_nu
            parts = [None] * 4
            for h in range(half_rows):
                term = (tiles_v[t, :, h * LANES:(h + 1) * LANES].astype(jnp.float32)
                        * weights[pl.ds(base + h, 1), :])
                parts[h % 4] = term if parts[h % 4] is None else parts[h % 4] + term
            totals.append((target, (parts[0] + parts[1]) + (parts[2] + parts[3])))
        for target, total in totals:
            sums[target] += total

    @pl.when(with_own)
    def _():
        pltpu.make_async_copy(tiles_hbm.at[pl.ds(0, EARLY)], tiles_v.at[pl.ds(0, EARLY)], sems.at[3]).wait()

    pl.loop(0, early_steps)(work)

    @pl.loop(early_number, number)
    def _(j):
        tile_copy(found[j]).wait()

    pl.loop(early_steps, steps)(work)


def own_first(sizes):
    return 2 * lax.axis_index("pair") < sizes[5]


def first_kernel(sizes, count_s, pairs_hbm, dom_hbm, coef_hbm, tiles_hbm,
                 own_keep, own_send, prior_keep, prior_send, *scratch):
    slab, domain_len, sums = sizes[2], sizes[3], scratch[-2]
    with_own = own_first(sizes)
    aux_id = lax.axis_index("aux")
    half_terms(sizes, 2 * slab, with_own, count_s, pairs_hbm, dom_hbm, coef_hbm, tiles_hbm, *scratch)
    fold(slab, domain_len, aux_id, lambda k: sums[slab * domain_len + k], prior_keep, prior_send)

    @pl.when(with_own)
    def _():
        fold(slab, domain_len, aux_id, lambda k: sums[k], own_keep, own_send)


def second_kernel(sizes, count_s, pairs_hbm, dom_hbm, coef_hbm, tiles_hbm, done_keep, done_send,
                  own_keep, own_send, *scratch):
    slab, domain_len, sums = sizes[2], sizes[3], scratch[-2]
    first = own_first(sizes)

    @pl.when(first)
    def _():
        own_keep[...] = done_keep[...]
        own_send[...] = done_send[...]

    @pl.when(jnp.logical_not(first))
    def _():
        half_terms(sizes, slab, jnp.logical_not(first), count_s, pairs_hbm, dom_hbm, coef_hbm, tiles_hbm, *scratch)
        fold(slab, domain_len, lax.axis_index("aux"), lambda k: sums[k], own_keep, own_send)


def fold(slab, domain_len, aux_id, read, keep, send):
    half = slab // 2
    for r in range(slab):
        first = lax.bitwise_xor(aux_id, r) * domain_len
        out = keep if r < half else send
        for u in range(domain_len // 2):
            left, right = read(first + 2 * u), read(first + 2 * u + 1)
            low = lax.broadcasted_iota(jnp.int32, left.shape, 1) < BLOCK
            out[r % half, :, u * LANES:(u + 1) * LANES] = (
                jnp.where(low, left, right) + pltpu.roll(jnp.where(low, right, left), BLOCK, 1)).astype(out.dtype)


def half_blocks(tile_values, tile_pairs, tile_counts, coeffs, domains, slab, pair_size):
    slots, aux_dev, flat = tile_values.shape
    orbitals = coeffs.shape[1]
    domain_len = domains.shape[1]
    own_blocks = coeffs.shape[0] // BLOCK
    hits_rows = (2 * slab + 8) // 8 * 8
    sizes = (slots, aux_dev, slab, domain_len, own_blocks, pair_size)
    out = jax.ShapeDtypeStruct((slab // 2, aux_dev, domain_len * BLOCK), jnp.float32)
    thin = jax.ShapeDtypeStruct(out.shape, jnp.bfloat16)
    vmem_spec = pl.BlockSpec(memory_space=pltpu.VMEM)
    any_spec = pl.BlockSpec(memory_space=pltpu.HBM)
    scratch = [
        pltpu.VMEM((2, slots), jnp.int32),
        pltpu.SMEM((domain_len, orbitals), jnp.int32),
        pltpu.VMEM((orbitals, own_blocks * BLOCK), jnp.bfloat16),
        pltpu.VMEM((own_blocks * BLOCK // LANES, orbitals, LANES), jnp.float32),
        pltpu.VMEM((slots, aux_dev, flat), jnp.bfloat16),
        pltpu.VMEM((hits_rows, LANES), jnp.int32),
        pltpu.SMEM((hits_rows, LANES), jnp.int32),
        pltpu.SMEM((slots + 1,), jnp.int32),
        pltpu.SMEM((2 * slab * slots + 2 * UNROLL,), jnp.int32),
        pltpu.VMEM((2, BLOCK // 2, LANES), jnp.float32),
        pltpu.VMEM((domain_len * BLOCK // 2, LANES), jnp.bfloat16),
        pltpu.VMEM(((2 * slab * domain_len + 1) * BLOCK // 2, LANES), jnp.float32),
        pltpu.VMEM((2 * slab * domain_len + 1, aux_dev, LANES), jnp.float32),
        pltpu.SemaphoreType.DMA((5,)),
    ]
    params = pltpu.CompilerParams(vmem_limit_bytes=16 * 1024 * 1024)
    smem_spec = pl.BlockSpec(memory_space=pltpu.SMEM)
    operands = [tile_counts] + [pltpu.with_memory_space_constraint(value, pltpu.HBM)
                                for value in (tile_pairs.T, domains.T, coeffs.T, tile_values)]
    done_keep, done_send, prior_keep, prior_send = pl.pallas_call(
        functools.partial(first_kernel, sizes),
        out_shape=[out, thin, thin, thin],
        in_specs=[smem_spec] + [any_spec] * 4,
        out_specs=[vmem_spec] * 4,
        scratch_shapes=scratch,
        compiler_params=params,
    )(*operands)
    own_keep, own_send = pl.pallas_call(
        functools.partial(second_kernel, sizes),
        out_shape=[out, thin],
        in_specs=[smem_spec] + [any_spec] * 4 + [vmem_spec] * 2,
        out_specs=[vmem_spec] * 2,
        scratch_shapes=scratch,
        compiler_params=params,
    )(*operands, done_keep, done_send)
    return own_keep, own_send, prior_keep, prior_send


def moved(value, aux_mask, pair_step):
    aux_size, pair_size = lax.axis_size("aux"), lax.axis_size("pair")
    routes = [
        (a * pair_size + p, (a ^ aux_mask) * pair_size + (p + pair_step) % pair_size)
        for a in range(aux_size)
        for p in range(pair_size)
    ]
    return lax.ppermute(value, ("aux", "pair"), routes)


def fit_kernel(sources, *refs):
    count = len(refs) - 3
    virtual, fitted, rows = refs[count:]
    aux_id = lax.axis_index("aux")
    height = refs[0].shape[1]
    for offset, ref, place in sources:
        start = pl.multiple_of(lax.bitwise_xor(aux_id, offset) * height, height)
        rows[pl.ds(start, height), :] = refs[ref][place].astype(jnp.float32)
    fitted[0] = jnp.dot(rows[...].astype(jnp.bfloat16), virtual[0],
                        preferred_element_type=jnp.float32).astype(fitted.dtype)


def body(tile_values, tile_pairs, tile_counts, coeffs, domains, virtual):
    pair_size = lax.axis_size("pair")
    aux_size = lax.axis_size("aux")
    slab = coeffs.shape[1] // pair_size
    aux_dev = tile_values.shape[1]
    own_keep, own_send, prior_keep, prior_send = half_blocks(tile_values, tile_pairs, tile_counts, coeffs, domains, slab, pair_size)

    half = aux_size // 2
    mask = half | 1
    prior_here = moved(prior_keep, 0, -1)
    prior_there = moved(prior_send, mask, -1)
    own_there = moved(own_send, mask, 0)
    prior_there, prior_here = lax.optimization_barrier((prior_there, prior_here))
    items = [((prior_here.astype(jnp.float32) + own_keep).astype(jnp.bfloat16), 0, 0),
             ((prior_there.astype(jnp.float32) + own_there.astype(jnp.float32)).astype(jnp.bfloat16), 1, mask)]
    while half > 2:
        half //= 2
        mask = half | 1
        sent = moved(jnp.concatenate([value[half:] for value, _, _ in items]), mask, 0)
        kept = [(value[:half], flip, source) for value, flip, source in items]
        got = [(sent[k * half:(k + 1) * half], flip ^ 1, source ^ mask) for k, (_, flip, source) in enumerate(items)]
        items = kept + got
    last = moved(jnp.concatenate([value[1 - flip:2 - flip] for value, flip, _ in items]), 1, 0)
    sources = []
    for k, (_, flip, source) in enumerate(items):
        sources.append((source, k, flip))
        sources.append((source ^ 1, len(items), k))
    arrays = [item[0] for item in items] + [last]
    return pl.pallas_call(
        functools.partial(fit_kernel, sources),
        out_shape=jax.ShapeDtypeStruct((1, aux_size * aux_dev, virtual.shape[2]), jnp.bfloat16),
        in_specs=[pl.BlockSpec(memory_space=pltpu.VMEM)] * (len(arrays) + 1),
        out_specs=pl.BlockSpec(memory_space=pltpu.VMEM),
        scratch_shapes=[pltpu.VMEM((aux_size * aux_dev, virtual.shape[1]), jnp.float32)],
        compiler_params=pltpu.CompilerParams(vmem_limit_bytes=4 * 1024 * 1024),
    )(*arrays, virtual)


def solution(mesh):
    placed = (
        P("pair", ("groups", "aux"), None),
        P("pair", None),
        P("pair"),
        P("pair", "groups"),
        P("groups", None),
        P(("groups", "pair", "aux"), None, None),
    )
    return jax.shard_map(
        body,
        mesh=mesh,
        in_specs=placed,
        out_specs=P(("pair", "aux"), "groups", None),
        check_vma=False,
    )
```

```python
import functools

import jax
import jax.numpy as jnp
from jax import lax
from jax.experimental import pallas as pl
from jax.experimental.pallas import tpu as pltpu
from jax.sharding import PartitionSpec as P

BLOCK = 64
LANES = 128
WORD = 32
UNROLL = 4
EARLY = 32
CHUNK = 4


def half_terms(sizes, orbitals, with_own, count_s, pairs_hbm, dom_hbm, coef_hbm, tiles_hbm,
               pairs_v, dom_s, coef_v, coef_f, tiles_v, hits_v, hits_s, found, todo,
               masks, picked, weights, sums, sems):
    slots, aux_dev, slab, domain_len, own_blocks, pair_size = sizes
    pair_id = lax.axis_index("pair")
    first_block = pair_id * own_blocks
    own_row = pair_id * slab
    prior_row = lax.rem(pair_id + pair_size - 1, pair_size) * slab
    half_rows = BLOCK // 2

    small = [
        pltpu.make_async_copy(dom_hbm, dom_s, sems.at[0]),
        pltpu.make_async_copy(pairs_hbm, pairs_v, sems.at[1]),
        pltpu.make_async_copy(coef_hbm, coef_v, sems.at[2]),
    ]
    for copy in small:
        copy.start()
    @pl.when(with_own)
    def _():
        for first in range(0, EARLY, CHUNK):
            pltpu.make_async_copy(
                tiles_hbm.at[pl.ds(first, CHUNK)], tiles_v.at[pl.ds(first, CHUNK)], sems.at[3]).start()


    row_i = lax.broadcasted_iota(jnp.int32, (half_rows, LANES), 0)
    lane_i = lax.broadcasted_iota(jnp.int32, (half_rows, LANES), 1)
    for e in range(2):
        masks[e] = (lax.shift_right_arithmetic(lane_i - e * BLOCK, 1) == row_i).astype(jnp.float32)
    src = lax.broadcasted_iota(jnp.int32, (LANES, LANES), 0)
    dst = lax.broadcasted_iota(jnp.int32, (LANES, LANES), 1)
    spread = ((src & 1) == lax.shift_right_logical(dst, 6)).astype(jnp.bfloat16)
    sums[...] = jnp.zeros_like(sums)
    weights[pl.ds(orbitals * domain_len * half_rows, half_rows), :] = jnp.zeros((half_rows, LANES), jnp.float32)

    for copy in small[:2]:
        copy.wait()

    def orbital_row(i):
        return own_row + i if i < slab else prior_row + i - slab

    slot_i = lax.broadcasted_iota(jnp.int32, (1, slots), 1)
    live = slot_i < count_s[0]
    mu = pairs_v[0:1, :]
    nu = pairs_v[1:2, :]
    taken = jnp.zeros((1, slots), jnp.int32)
    coded = [jnp.zeros((1, slots), jnp.int32) for _ in range(orbitals)]
    for i in range(orbitals):
        row = orbital_row(i)
        at_mu = jnp.full((1, slots), -1, jnp.int32)
        at_nu = jnp.full((1, slots), -1, jnp.int32)
        for s in range(domain_len):
            block = dom_s[s, row]
            at_mu = jnp.where(mu == block, s, at_mu)
            at_nu = jnp.where(nu == block, s, at_nu)
        hit = (live & with_own if i < slab else live) & (at_mu >= 0) & (at_nu >= 0)
        code = (i * domain_len + at_mu) * domain_len + at_nu
        for k in range(i + 1):
            coded[k] = jnp.where(hit & (taken == k), code, coded[k])
        taken = taken + hit.astype(jnp.int32)
    for k in range(orbitals):
        hits_v[k:k + 1, 0:slots] = coded[k]
    hits_v[orbitals:orbitals + 1, 0:slots] = taken
    hits_copy = pltpu.make_async_copy(hits_v, hits_s, sems.at[0])
    hits_copy.start()

    number = jnp.int32(0)
    early_number = number
    for first in range(0, slots, WORD):
        inside = (taken > 0) & (slot_i >= first) & (slot_i < first + WORD)
        word = jnp.sum(jnp.where(inside, lax.shift_left(1, slot_i & (WORD - 1)), 0))
        for t in range(WORD):
            if first + t == EARLY:
                early_number = number
            found[number] = first + t
            number = number + (lax.shift_right_logical(word, t) & 1)

    early_number = jnp.where(with_own, early_number, 0)

    def tile_copy(t):
        return pltpu.make_async_copy(tiles_hbm.at[t], tiles_v.at[t], sems.at[4])

    @pl.loop(early_number, number)
    def _(j):
        tile_copy(found[j]).start()

    small[2].wait()
    for e in range(own_blocks // 2):
        coef_f[e] = coef_v[:, e * LANES:(e + 1) * LANES].astype(jnp.float32)

    for i in range(orbitals):
        row = orbital_row(i)
        for s in range(domain_len):
            local = jnp.clip(dom_s[s, row] - first_block, 0, own_blocks - 1)
            line = coef_f[lax.shift_right_logical(local, 1), pl.ds(row, 1), :]
            picked[pl.ds(s * half_rows, half_rows), :] = (masks[local & 1] * line).astype(jnp.bfloat16)
        weights[pl.ds(i * domain_len * half_rows, domain_len * half_rows), :] = jnp.dot(
            picked[...], spread, preferred_element_type=jnp.float32)

    hits_copy.wait()

    def listed(j, filled):
        t = found[j]

        def entry(k, at):
            todo[at] = hits_s[k, t] * slots + t
            return at + 1

        return lax.fori_loop(0, hits_s[orbitals, t], entry, filled)

    nothing = orbitals * domain_len * domain_len * slots
    early_hits = lax.fori_loop(0, early_number, listed, jnp.int32(0))
    for u in range(UNROLL - 1):
        todo[early_hits + u] = nothing
    early_steps = lax.div(early_hits + UNROLL - 1, UNROLL)
    hits = lax.fori_loop(early_number, number, listed, early_steps * UNROLL)
    for u in range(UNROLL - 1):
        todo[hits + u] = nothing
    steps = lax.div(hits + UNROLL - 1, UNROLL)

    def work(step):
        totals = []
        for u in range(UNROLL):
            word = todo[step * UNROLL + u]
            t = word & (slots - 1)
            code = lax.div(word, slots)
            at_nu = lax.rem(code, domain_len)
            source = lax.div(code, domain_len)
            base = source * half_rows
            target = lax.div(source, domain_len) * domain_len + at_nu
            parts = [None] * 4
            for h in range(half_rows):
                term = (tiles_v[t, :, h * LANES:(h + 1) * LANES].astype(jnp.float32)
                        * weights[pl.ds(base + h, 1), :])
                parts[h % 4] = term if parts[h % 4] is None else parts[h % 4] + term
            totals.append((target, (parts[0] + parts[1]) + (parts[2] + parts[3])))
        for target, total in totals:
            sums[target] += total

    @pl.when(with_own)
    def _():
        pltpu.make_async_copy(tiles_hbm.at[pl.ds(0, EARLY)], tiles_v.at[pl.ds(0, EARLY)], sems.at[3]).wait()

    pl.loop(0, early_steps)(work)

    @pl.loop(early_number, number)
    def _(j):
        tile_copy(found[j]).wait()

    pl.loop(early_steps, steps)(work)


def own_first(sizes):
    return 2 * lax.axis_index("pair") < sizes[5]


def first_kernel(sizes, count_s, pairs_hbm, dom_hbm, coef_hbm, tiles_hbm,
                 own_keep, own_send, prior_keep, prior_send, *scratch):
    slab, domain_len, sums = sizes[2], sizes[3], scratch[-2]
    with_own = own_first(sizes)
    aux_id = lax.axis_index("aux")
    half_terms(sizes, 2 * slab, with_own, count_s, pairs_hbm, dom_hbm, coef_hbm, tiles_hbm, *scratch)
    fold(slab, domain_len, aux_id, lambda k: sums[slab * domain_len + k], prior_keep, prior_send)

    @pl.when(with_own)
    def _():
        fold(slab, domain_len, aux_id, lambda k: sums[k], own_keep, own_send)


def second_kernel(sizes, count_s, pairs_hbm, dom_hbm, coef_hbm, tiles_hbm, done_keep, done_send,
                  own_keep, own_send, *scratch):
    slab, domain_len, sums = sizes[2], sizes[3], scratch[-2]
    first = own_first(sizes)

    @pl.when(first)
    def _():
        own_keep[...] = done_keep[...]
        own_send[...] = done_send[...]

    @pl.when(jnp.logical_not(first))
    def _():
        half_terms(sizes, slab, jnp.logical_not(first), count_s, pairs_hbm, dom_hbm, coef_hbm, tiles_hbm, *scratch)
        fold(slab, domain_len, lax.axis_index("aux"), lambda k: sums[k], own_keep, own_send)


def fold(slab, domain_len, aux_id, read, keep, send):
    half = slab // 2
    for r in range(slab):
        first = lax.bitwise_xor(aux_id, r) * domain_len
        out = keep if r < half else send
        for u in range(domain_len // 2):
            left, right = read(first + 2 * u), read(first + 2 * u + 1)
            low = lax.broadcasted_iota(jnp.int32, left.shape, 1) < BLOCK
            out[r % half, :, u * LANES:(u + 1) * LANES] = (
                jnp.where(low, left, right) + pltpu.roll(jnp.where(low, right, left), BLOCK, 1)).astype(out.dtype)


def half_blocks(tile_values, tile_pairs, tile_counts, coeffs, domains, slab, pair_size):
    slots, aux_dev, flat = tile_values.shape
    orbitals = coeffs.shape[1]
    domain_len = domains.shape[1]
    own_blocks = coeffs.shape[0] // BLOCK
    hits_rows = (2 * slab + 8) // 8 * 8
    sizes = (slots, aux_dev, slab, domain_len, own_blocks, pair_size)
    out = jax.ShapeDtypeStruct((slab // 2, aux_dev, domain_len * BLOCK), jnp.float32)
    thin = jax.ShapeDtypeStruct(out.shape, jnp.bfloat16)
    vmem_spec = pl.BlockSpec(memory_space=pltpu.VMEM)
    any_spec = pl.BlockSpec(memory_space=pltpu.HBM)
    scratch = [
        pltpu.VMEM((2, slots), jnp.int32),
        pltpu.SMEM((domain_len, orbitals), jnp.int32),
        pltpu.VMEM((orbitals, own_blocks * BLOCK), jnp.bfloat16),
        pltpu.VMEM((own_blocks * BLOCK // LANES, orbitals, LANES), jnp.float32),
        pltpu.VMEM((slots, aux_dev, flat), jnp.bfloat16),
        pltpu.VMEM((hits_rows, LANES), jnp.int32),
        pltpu.SMEM((hits_rows, LANES), jnp.int32),
        pltpu.SMEM((slots + 1,), jnp.int32),
        pltpu.SMEM((2 * slab * slots + 2 * UNROLL,), jnp.int32),
        pltpu.VMEM((2, BLOCK // 2, LANES), jnp.float32),
        pltpu.VMEM((domain_len * BLOCK // 2, LANES), jnp.bfloat16),
        pltpu.VMEM(((2 * slab * domain_len + 1) * BLOCK // 2, LANES), jnp.float32),
        pltpu.VMEM((2 * slab * domain_len + 1, aux_dev, LANES), jnp.float32),
        pltpu.SemaphoreType.DMA((5,)),
    ]
    params = pltpu.CompilerParams(vmem_limit_bytes=16 * 1024 * 1024)
    smem_spec = pl.BlockSpec(memory_space=pltpu.SMEM)
    operands = [tile_counts] + [pltpu.with_memory_space_constraint(value, pltpu.HBM)
                                for value in (tile_pairs.T, domains.T, coeffs.T, tile_values)]
    done_keep, done_send, prior_keep, prior_send = pl.pallas_call(
        functools.partial(first_kernel, sizes),
        out_shape=[out, thin, thin, thin],
        in_specs=[smem_spec] + [any_spec] * 4,
        out_specs=[vmem_spec] * 4,
        scratch_shapes=scratch,
        compiler_params=params,
    )(*operands)
    own_keep, own_send = pl.pallas_call(
        functools.partial(second_kernel, sizes),
        out_shape=[out, thin],
        in_specs=[smem_spec] + [any_spec] * 4 + [vmem_spec] * 2,
        out_specs=[vmem_spec] * 2,
        scratch_shapes=scratch,
        compiler_params=params,
    )(*operands, done_keep, done_send)
    return own_keep, own_send, prior_keep, prior_send


def moved(value, aux_mask, pair_step):
    aux_size, pair_size = lax.axis_size("aux"), lax.axis_size("pair")
    routes = [
        (a * pair_size + p, (a ^ aux_mask) * pair_size + (p + pair_step) % pair_size)
        for a in range(aux_size)
        for p in range(pair_size)
    ]
    return lax.ppermute(value, ("aux", "pair"), routes)


def fit_rows(blocks, virtual):
    rows = jnp.concatenate([block.astype(jnp.float32) for block in blocks])
    return jnp.dot(rows.astype(jnp.bfloat16), virtual[0], preferred_element_type=jnp.float32)


def kept_kernel(flips, *refs):
    virtual, part = refs[-2:]
    part[...] = fit_rows([ref[flip] for ref, flip in zip(refs, flips)], virtual)


def swapped_kernel(offsets, part, last, virtual, fitted, rows):
    aux_id = lax.axis_index("aux")
    height = last.shape[1]
    other = fit_rows([last[k] for k in range(len(offsets))], virtual)
    for k, offset in enumerate(offsets):
        for values, source in ((part, offset), (other, offset ^ 1)):
            start = pl.multiple_of(lax.bitwise_xor(aux_id, source) * height, height)
            rows[pl.ds(start, height), :] = values[k * height:(k + 1) * height]
    fitted[0] = rows[...].astype(fitted.dtype)


def body(tile_values, tile_pairs, tile_counts, coeffs, domains, virtual):
    pair_size = lax.axis_size("pair")
    aux_size = lax.axis_size("aux")
    slab = coeffs.shape[1] // pair_size
    aux_dev = tile_values.shape[1]
    own_keep, own_send, prior_keep, prior_send = half_blocks(tile_values, tile_pairs, tile_counts, coeffs, domains, slab, pair_size)

    half = aux_size // 2
    mask = half | 1
    prior_here = moved(prior_keep, 0, -1)
    prior_there = moved(prior_send, mask, -1)
    own_there = moved(own_send, mask, 0)
    prior_there, prior_here = lax.optimization_barrier((prior_there, prior_here))
    items = [((prior_here.astype(jnp.float32) + own_keep).astype(jnp.bfloat16), 0, 0),
             ((prior_there.astype(jnp.float32) + own_there.astype(jnp.float32)).astype(jnp.bfloat16), 1, mask)]
    while half > 2:
        half //= 2
        mask = half | 1
        sent = moved(jnp.concatenate([value[half:] for value, _, _ in items]), mask, 0)
        kept = [(value[:half], flip, source) for value, flip, source in items]
        got = [(sent[k * half:(k + 1) * half], flip ^ 1, source ^ mask) for k, (_, flip, source) in enumerate(items)]
        items = kept + got
    last = moved(jnp.concatenate([value[1 - flip:2 - flip] for value, flip, _ in items]), 1, 0)
    vmem_spec = pl.BlockSpec(memory_space=pltpu.VMEM)
    params = pltpu.CompilerParams(vmem_limit_bytes=4 * 1024 * 1024)
    width = virtual.shape[2]
    part = pl.pallas_call(
        functools.partial(kept_kernel, [flip for _, flip, _ in items]),
        out_shape=jax.ShapeDtypeStruct((len(items) * aux_dev, width), jnp.float32),
        in_specs=[vmem_spec] * (len(items) + 1),
        out_specs=vmem_spec,
        compiler_params=params,
    )(*[value for value, _, _ in items], virtual)
    return pl.pallas_call(
        functools.partial(swapped_kernel, [source for _, _, source in items]),
        out_shape=jax.ShapeDtypeStruct((1, aux_size * aux_dev, width), jnp.bfloat16),
        in_specs=[vmem_spec] * 3,
        out_specs=vmem_spec,
        scratch_shapes=[pltpu.VMEM((aux_size * aux_dev, width), jnp.float32)],
        compiler_params=params,
    )(part, last, virtual)


def solution(mesh):
    placed = (
        P("pair", ("groups", "aux"), None),
        P("pair", None),
        P("pair"),
        P("pair", "groups"),
        P("groups", None),
        P(("groups", "pair", "aux"), None, None),
    )
    return jax.shard_map(
        body,
        mesh=mesh,
        in_specs=placed,
        out_specs=P(("pair", "aux"), "groups", None),
        check_vma=False,
    )
```

```python
import functools

import jax
import jax.numpy as jnp
from jax import lax
from jax.experimental import pallas as pl
from jax.experimental.pallas import tpu as pltpu
from jax.sharding import PartitionSpec as P

BLOCK = 64
LANES = 128
WORD = 32
UNROLL = 4
EARLY = 32
CHUNK = 4


def half_terms(sizes, orbitals, with_own, count_s, pairs_hbm, dom_hbm, coef_hbm, tiles_hbm,
               pairs_v, dom_s, coef_v, coef_f, tiles_v, hits_v, hits_s, found, todo,
               masks, picked, weights, sums, sems):
    slots, aux_dev, slab, domain_len, own_blocks, pair_size = sizes
    pair_id = lax.axis_index("pair")
    first_block = pair_id * own_blocks
    own_row = pair_id * slab
    prior_row = lax.rem(pair_id + pair_size - 1, pair_size) * slab
    half_rows = BLOCK // 2

    small = [
        pltpu.make_async_copy(dom_hbm, dom_s, sems.at[0]),
        pltpu.make_async_copy(pairs_hbm, pairs_v, sems.at[1]),
        pltpu.make_async_copy(coef_hbm, coef_v, sems.at[2]),
    ]
    for copy in small:
        copy.start()
    @pl.when(with_own)
    def _():
        for first in range(0, EARLY, CHUNK):
            pltpu.make_async_copy(
                tiles_hbm.at[pl.ds(first, CHUNK)], tiles_v.at[pl.ds(first, CHUNK)], sems.at[3]).start()


    row_i = lax.broadcasted_iota(jnp.int32, (half_rows, LANES), 0)
    lane_i = lax.broadcasted_iota(jnp.int32, (half_rows, LANES), 1)
    for e in range(2):
        masks[e] = (lax.shift_right_arithmetic(lane_i - e * BLOCK, 1) == row_i).astype(jnp.float32)
    src = lax.broadcasted_iota(jnp.int32, (LANES, LANES), 0)
    dst = lax.broadcasted_iota(jnp.int32, (LANES, LANES), 1)
    spread = ((src & 1) == lax.shift_right_logical(dst, 6)).astype(jnp.bfloat16)
    sums[...] = jnp.zeros_like(sums)
    weights[pl.ds(orbitals * domain_len * half_rows, half_rows), :] = jnp.zeros((half_rows, LANES), jnp.float32)

    for copy in small[:2]:
        copy.wait()

    def orbital_row(i):
        return own_row + i if i < slab else prior_row + i - slab

    slot_i = lax.broadcasted_iota(jnp.int32, (1, slots), 1)
    live = slot_i < count_s[0]
    mu = pairs_v[0:1, :]
    nu = pairs_v[1:2, :]
    taken = jnp.zeros((1, slots), jnp.int32)
    coded = [jnp.zeros((1, slots), jnp.int32) for _ in range(orbitals)]
    for i in range(orbitals):
        row = orbital_row(i)
        at_mu = jnp.full((1, slots), -1, jnp.int32)
        at_nu = jnp.full((1, slots), -1, jnp.int32)
        for s in range(domain_len):
            block = dom_s[s, row]
            at_mu = jnp.where(mu == block, s, at_mu)
            at_nu = jnp.where(nu == block, s, at_nu)
        hit = (live & with_own if i < slab else live) & (at_mu >= 0) & (at_nu >= 0)
        code = (i * domain_len + at_mu) * domain_len + at_nu
        for k in range(i + 1):
            coded[k] = jnp.where(hit & (taken == k), code, coded[k])
        taken = taken + hit.astype(jnp.int32)
    for k in range(orbitals):
        hits_v[k:k + 1, 0:slots] = coded[k]
    hits_v[orbitals:orbitals + 1, 0:slots] = taken
    hits_copy = pltpu.make_async_copy(hits_v, hits_s, sems.at[0])
    hits_copy.start()

    number = jnp.int32(0)
    early_number = number
    for first in range(0, slots, WORD):
        inside = (taken > 0) & (slot_i >= first) & (slot_i < first + WORD)
        word = jnp.sum(jnp.where(inside, lax.shift_left(1, slot_i & (WORD - 1)), 0))
        for t in range(WORD):
            if first + t == EARLY:
                early_number = number
            found[number] = first + t
            number = number + (lax.shift_right_logical(word, t) & 1)

    early_number = jnp.where(with_own, early_number, 0)

    def tile_copy(t):
        return pltpu.make_async_copy(tiles_hbm.at[t], tiles_v.at[t], sems.at[4])

    @pl.loop(early_number, number)
    def _(j):
        tile_copy(found[j]).start()

    small[2].wait()
    for e in range(own_blocks // 2):
        coef_f[e] = coef_v[:, e * LANES:(e + 1) * LANES].astype(jnp.float32)

    def weigh(i):
        row = orbital_row(i)
        for s in range(domain_len):
            local = jnp.clip(dom_s[s, row] - first_block, 0, own_blocks - 1)
            line = coef_f[lax.shift_right_logical(local, 1), pl.ds(row, 1), :]
            picked[pl.ds(s * half_rows, half_rows), :] = (masks[local & 1] * line).astype(jnp.bfloat16)
        weights[pl.ds(i * domain_len * half_rows, domain_len * half_rows), :] = jnp.dot(
            picked[...], spread, preferred_element_type=jnp.float32)

    for i in range(slab, orbitals):
        weigh(i)

    @pl.when(with_own)
    def _():
        for i in range(slab):
            weigh(i)

    hits_copy.wait()

    def listed(j, filled):
        t = found[j]

        def entry(k, at):
            todo[at] = hits_s[k, t] * slots + t
            return at + 1

        return lax.fori_loop(0, hits_s[orbitals, t], entry, filled)

    nothing = orbitals * domain_len * domain_len * slots
    early_hits = lax.fori_loop(0, early_number, listed, jnp.int32(0))
    for u in range(UNROLL - 1):
        todo[early_hits + u] = nothing
    early_steps = lax.div(early_hits + UNROLL - 1, UNROLL)
    hits = lax.fori_loop(early_number, number, listed, early_steps * UNROLL)
    for u in range(UNROLL - 1):
        todo[hits + u] = nothing
    steps = lax.div(hits + UNROLL - 1, UNROLL)

    def work(step):
        totals = []
        for u in range(UNROLL):
            word = todo[step * UNROLL + u]
            t = word & (slots - 1)
            code = lax.div(word, slots)
            at_nu = lax.rem(code, domain_len)
            source = lax.div(code, domain_len)
            base = source * half_rows
            target = lax.div(source, domain_len) * domain_len + at_nu
            parts = [None] * 4
            for h in range(half_rows):
                term = (tiles_v[t, :, h * LANES:(h + 1) * LANES].astype(jnp.float32)
                        * weights[pl.ds(base + h, 1), :])
                parts[h % 4] = term if parts[h % 4] is None else parts[h % 4] + term
            totals.append((target, (parts[0] + parts[1]) + (parts[2] + parts[3])))
        for target, total in totals:
            sums[target] += total

    @pl.when(with_own)
    def _():
        pltpu.make_async_copy(tiles_hbm.at[pl.ds(0, EARLY)], tiles_v.at[pl.ds(0, EARLY)], sems.at[3]).wait()

    pl.loop(0, early_steps)(work)

    @pl.loop(early_number, number)
    def _(j):
        tile_copy(found[j]).wait()

    pl.loop(early_steps, steps)(work)


def own_first(sizes):
    return 2 * lax.axis_index("pair") < sizes[5]


def first_kernel(sizes, count_s, pairs_hbm, dom_hbm, coef_hbm, tiles_hbm,
                 own_keep, own_send, prior_keep, prior_send, *scratch):
    slab, domain_len, sums = sizes[2], sizes[3], scratch[-2]
    with_own = own_first(sizes)
    aux_id = lax.axis_index("aux")
    half_terms(sizes, 2 * slab, with_own, count_s, pairs_hbm, dom_hbm, coef_hbm, tiles_hbm, *scratch)
    fold(slab, domain_len, aux_id, lambda k: sums[slab * domain_len + k], prior_keep, prior_send)

    @pl.when(with_own)
    def _():
        fold(slab, domain_len, aux_id, lambda k: sums[k], own_keep, own_send)


def second_kernel(sizes, count_s, pairs_hbm, dom_hbm, coef_hbm, tiles_hbm, done_keep, done_send,
                  own_keep, own_send, *scratch):
    slab, domain_len, sums = sizes[2], sizes[3], scratch[-2]
    first = own_first(sizes)

    @pl.when(first)
    def _():
        own_keep[...] = done_keep[...]
        own_send[...] = done_send[...]

    @pl.when(jnp.logical_not(first))
    def _():
        half_terms(sizes, slab, jnp.logical_not(first), count_s, pairs_hbm, dom_hbm, coef_hbm, tiles_hbm, *scratch)
        fold(slab, domain_len, lax.axis_index("aux"), lambda k: sums[k], own_keep, own_send)


def fold(slab, domain_len, aux_id, read, keep, send):
    half = slab // 2
    for r in range(slab):
        first = lax.bitwise_xor(aux_id, r) * domain_len
        out = keep if r < half else send
        for u in range(domain_len // 2):
            left, right = read(first + 2 * u), read(first + 2 * u + 1)
            low = lax.broadcasted_iota(jnp.int32, left.shape, 1) < BLOCK
            out[r % half, :, u * LANES:(u + 1) * LANES] = (
                jnp.where(low, left, right) + pltpu.roll(jnp.where(low, right, left), BLOCK, 1)).astype(out.dtype)


def half_blocks(tile_values, tile_pairs, tile_counts, coeffs, domains, slab, pair_size):
    slots, aux_dev, flat = tile_values.shape
    orbitals = coeffs.shape[1]
    domain_len = domains.shape[1]
    own_blocks = coeffs.shape[0] // BLOCK
    hits_rows = (2 * slab + 8) // 8 * 8
    sizes = (slots, aux_dev, slab, domain_len, own_blocks, pair_size)
    out = jax.ShapeDtypeStruct((slab // 2, aux_dev, domain_len * BLOCK), jnp.float32)
    thin = jax.ShapeDtypeStruct(out.shape, jnp.bfloat16)
    vmem_spec = pl.BlockSpec(memory_space=pltpu.VMEM)
    any_spec = pl.BlockSpec(memory_space=pltpu.HBM)
    scratch = [
        pltpu.VMEM((2, slots), jnp.int32),
        pltpu.SMEM((domain_len, orbitals), jnp.int32),
        pltpu.VMEM((orbitals, own_blocks * BLOCK), jnp.bfloat16),
        pltpu.VMEM((own_blocks * BLOCK // LANES, orbitals, LANES), jnp.float32),
        pltpu.VMEM((slots, aux_dev, flat), jnp.bfloat16),
        pltpu.VMEM((hits_rows, LANES), jnp.int32),
        pltpu.SMEM((hits_rows, LANES), jnp.int32),
        pltpu.SMEM((slots + 1,), jnp.int32),
        pltpu.SMEM((2 * slab * slots + 2 * UNROLL,), jnp.int32),
        pltpu.VMEM((2, BLOCK // 2, LANES), jnp.float32),
        pltpu.VMEM((domain_len * BLOCK // 2, LANES), jnp.bfloat16),
        pltpu.VMEM(((2 * slab * domain_len + 1) * BLOCK // 2, LANES), jnp.float32),
        pltpu.VMEM((2 * slab * domain_len + 1, aux_dev, LANES), jnp.float32),
        pltpu.SemaphoreType.DMA((5,)),
    ]
    params = pltpu.CompilerParams(vmem_limit_bytes=16 * 1024 * 1024)
    smem_spec = pl.BlockSpec(memory_space=pltpu.SMEM)
    operands = [tile_counts] + [pltpu.with_memory_space_constraint(value, pltpu.HBM)
                                for value in (tile_pairs.T, domains.T, coeffs.T, tile_values)]
    done_keep, done_send, prior_keep, prior_send = pl.pallas_call(
        functools.partial(first_kernel, sizes),
        out_shape=[out, thin, thin, thin],
        in_specs=[smem_spec] + [any_spec] * 4,
        out_specs=[vmem_spec] * 4,
        scratch_shapes=scratch,
        compiler_params=params,
    )(*operands)
    own_keep, own_send = pl.pallas_call(
        functools.partial(second_kernel, sizes),
        out_shape=[out, thin],
        in_specs=[smem_spec] + [any_spec] * 4 + [vmem_spec] * 2,
        out_specs=[vmem_spec] * 2,
        scratch_shapes=scratch,
        compiler_params=params,
    )(*operands, done_keep, done_send)
    return own_keep, own_send, prior_keep, prior_send


def moved(value, aux_mask, pair_step):
    aux_size, pair_size = lax.axis_size("aux"), lax.axis_size("pair")
    routes = [
        (a * pair_size + p, (a ^ aux_mask) * pair_size + (p + pair_step) % pair_size)
        for a in range(aux_size)
        for p in range(pair_size)
    ]
    return lax.ppermute(value, ("aux", "pair"), routes)


def fit_rows(blocks, virtual):
    rows = jnp.concatenate([block.astype(jnp.float32) for block in blocks])
    return jnp.dot(rows.astype(jnp.bfloat16), virtual[0], preferred_element_type=jnp.float32)


def kept_kernel(flips, *refs):
    virtual, part = refs[-2:]
    part[...] = fit_rows([ref[flip] for ref, flip in zip(refs, flips)], virtual)


def swapped_kernel(offsets, part, last, virtual, fitted, rows):
    aux_id = lax.axis_index("aux")
    height = last.shape[1]
    other = fit_rows([last[k] for k in range(len(offsets))], virtual)
    for k, offset in enumerate(offsets):
        for values, source in ((part, offset), (other, offset ^ 1)):
            start = pl.multiple_of(lax.bitwise_xor(aux_id, source) * height, height)
            rows[pl.ds(start, height), :] = values[k * height:(k + 1) * height]
    fitted[0] = rows[...].astype(fitted.dtype)


def body(tile_values, tile_pairs, tile_counts, coeffs, domains, virtual):
    pair_size = lax.axis_size("pair")
    aux_size = lax.axis_size("aux")
    slab = coeffs.shape[1] // pair_size
    aux_dev = tile_values.shape[1]
    own_keep, own_send, prior_keep, prior_send = half_blocks(tile_values, tile_pairs, tile_counts, coeffs, domains, slab, pair_size)

    half = aux_size // 2
    mask = half | 1
    prior_here = moved(prior_keep, 0, -1)
    prior_there = moved(prior_send, mask, -1)
    own_there = moved(own_send, mask, 0)
    prior_there, prior_here = lax.optimization_barrier((prior_there, prior_here))
    items = [((prior_here.astype(jnp.float32) + own_keep).astype(jnp.bfloat16), 0, 0),
             ((prior_there.astype(jnp.float32) + own_there.astype(jnp.float32)).astype(jnp.bfloat16), 1, mask)]
    while half > 2:
        half //= 2
        mask = half | 1
        sent = moved(jnp.concatenate([value[half:] for value, _, _ in items]), mask, 0)
        kept = [(value[:half], flip, source) for value, flip, source in items]
        got = [(sent[k * half:(k + 1) * half], flip ^ 1, source ^ mask) for k, (_, flip, source) in enumerate(items)]
        items = kept + got
    last = moved(jnp.concatenate([value[1 - flip:2 - flip] for value, flip, _ in items]), 1, 0)
    vmem_spec = pl.BlockSpec(memory_space=pltpu.VMEM)
    params = pltpu.CompilerParams(vmem_limit_bytes=4 * 1024 * 1024)
    width = virtual.shape[2]
    part = pl.pallas_call(
        functools.partial(kept_kernel, [flip for _, flip, _ in items]),
        out_shape=jax.ShapeDtypeStruct((len(items) * aux_dev, width), jnp.float32),
        in_specs=[vmem_spec] * (len(items) + 1),
        out_specs=vmem_spec,
        compiler_params=params,
    )(*[value for value, _, _ in items], virtual)
    return pl.pallas_call(
        functools.partial(swapped_kernel, [source for _, _, source in items]),
        out_shape=jax.ShapeDtypeStruct((1, aux_size * aux_dev, width), jnp.bfloat16),
        in_specs=[vmem_spec] * 3,
        out_specs=vmem_spec,
        scratch_shapes=[pltpu.VMEM((aux_size * aux_dev, width), jnp.float32)],
        compiler_params=params,
    )(part, last, virtual)


def solution(mesh):
    placed = (
        P("pair", ("groups", "aux"), None),
        P("pair", None),
        P("pair"),
        P("pair", "groups"),
        P("groups", None),
        P(("groups", "pair", "aux"), None, None),
    )
    return jax.shard_map(
        body,
        mesh=mesh,
        in_specs=placed,
        out_specs=P(("pair", "aux"), "groups", None),
        check_vma=False,
    )
```
